32 devices in a mesh: row: 4 (over y, x), col: 8 (over z, core).
Axes of the slice: x: 2, y: 2, z: 4, core: 2. Of those that a mesh axis runs over, the one named last changes fastest.
Arguments:
- omega_sq: float32 [8192, 8192], P('row', 'col'), may hold values from -6 to 6
- pole_freq: float32 [8192, 8192], P('row', 'col'), may hold values from 0.5 to 4
- mtx_left: float32 [1, 8192, 128], P(None, ('row', 'col')), may hold values from -0.0625 to 0.0625
- mtx_right: float32 [1, 8192, 128], P(None, ('col', 'row')), may hold values from -0.0625 to 0.0625
- band_ids: int32 [1], replicated, may hold values from 0 to 63
- band_energy: float32 [64], replicated, may hold values from -3 to 1
- eval_energy: float32 [3], replicated, may hold values from -1 to 1
Outputs:
- sigma: float32 [128, 384], replicated
The draws below stay inside these ranges and needn't reach their ends.
All inputs are finite; a program needn't handle non-finite values.
Results may differ from the reference program's by a relative error of at most 0.0001.
Values sent between devices are 32-bit elements; how exact they have to be, the bound alone decides.
A program may use at most 64 MiB of HBM per device.

```python
import math
import jax
import jax.numpy as jnp
from jax import lax

NG = 8192
NS = 128
NE = 3
NBAND = 1
NSTORE = 64


def steps_of(key, shape, cuts, low, top_value):
    level = 1.0
    for position, blocks in cuts:
        heights = jax.random.uniform(jax.random.fold_in(jax.random.fold_in(key, 6), position), (blocks,), jnp.float32, low / len(cuts), top_value / len(cuts))
        level = level * jnp.repeat(jnp.exp(heights), shape[position] // blocks).reshape((-1,) + (1,) * (len(shape) - 1 - position))
    return level


def normal_values(key, extent, width, bound, shards=(), held_as=jnp.bfloat16):
    values = jax.random.normal(key, extent, jnp.float32) * width
    if len(shards) > 0:
        values = steps_of(key, extent, shards, -0.22, 0.18) * values
    return jnp.clip(values, min=-bound, max=bound).astype(held_as)


def setup_inputs(seed: int = 0) -> dict:
    arg_keys = jax.random.split(jax.random.key(seed), 8)
    return {
        "omega_sq": normal_values(arg_keys[0], (NG, NG), 1.0, 6.0, ((0, 4), (1, 8)), jnp.float32),
        "pole_freq": jnp.clip(jnp.exp(math.log(4.0) - 2.0794415 * jax.random.uniform(arg_keys[1], (NG, NG), jnp.float32) ** steps_of(arg_keys[1], (NG, NG), ((0, 4), (1, 8)), -0.2, 0.2)), 0.5, 4.0),
        "mtx_left": normal_values(arg_keys[2], (NBAND, NG, NS), NG ** -0.5, 0.0625, ((1, 32),), jnp.float32),
        "mtx_right": normal_values(arg_keys[3], (NBAND, NG, NS), NG ** -0.5, 0.0625, ((1, 32),), jnp.float32),
        "band_ids": jax.random.randint(arg_keys[4], (NBAND,), 0, NSTORE).astype(jnp.int32),
        "band_energy": jnp.clip(jax.random.uniform(arg_keys[5], (NSTORE,), jnp.float32, -3.0, 1.0), -3.0, 1.0),
        "eval_energy": jnp.clip(jax.random.uniform(arg_keys[6], (NE,), jnp.float32, -1.0, 1.0), -1.0, 1.0),
    }


def reference(omega_sq, pole_freq, mtx_left, mtx_right, band_ids, band_energy, eval_energy):
    hits = (band_ids[:, None] == jnp.arange(band_energy.shape[0], dtype=jnp.int32)[None, :]).astype(band_energy.dtype)
    levels = jnp.sum(hits * band_energy[None, :], axis=1)
    shifts = eval_energy[None, :] - levels[:, None]
    blocks = 16
    rows = NG // blocks
    omega_blocks = omega_sq.reshape(blocks, rows, NG)
    freq_blocks = pole_freq.reshape(blocks, rows, NG)
    left_blocks = jnp.transpose(mtx_left.reshape(NBAND, blocks, rows, NS), (1, 0, 2, 3))

    def step(total, pieces):
        omega_rows, freq_rows, left_rows = pieces
        ratio = omega_rows / freq_rows
        for band in range(NBAND):
            parts = []
            for energy in range(NE):
                gap = shifts[band, energy] - freq_rows
                kern = ratio * gap / (gap * gap + 0.09)
                parts.append(jnp.dot(kern, mtx_right[band], preferred_element_type=jnp.float32, precision=lax.Precision.HIGHEST))
            product = jnp.concatenate(parts, axis=1)
            total = total + lax.dot_general(left_rows[band], product, (((0,), (0,)), ((), ())), precision=lax.Precision.HIGHEST, preferred_element_type=jnp.float32)
        return total, None

    start = jnp.zeros((NS, NE * NS), omega_sq.dtype)
    total, unused = lax.scan(step, start, (omega_blocks, freq_blocks, left_blocks))
    return total
```

```python
import functools

import jax
import jax.numpy as jnp
from jax import lax
from jax.experimental import pallas as pl
from jax.experimental.pallas import tpu as pltpu
from jax.sharding import PartitionSpec as P

MESH = pl.DeviceIdType.MESH
F32 = jnp.float32
BF16 = jnp.bfloat16


def contract_rows(left, right):
    return lax.dot_general(
        left,
        right,
        (((0,), (0,)), ((), ())),
        precision=lax.Precision.HIGHEST,
        preferred_element_type=F32,
    )


def plain(omega_sq, pole_freq, mtx_left, mtx_right, band_ids, band_energy, eval_energy):
    shifts = eval_energy - band_energy[band_ids[0]]
    ratio = omega_sq / pole_freq
    right_cols = lax.all_gather(mtx_right[0], "row", axis=0, tiled=True)
    parts = []
    for energy in range(eval_energy.shape[0]):
        gap = shifts[energy] - pole_freq
        kern = ratio * gap / (gap * gap + 0.09)
        parts.append(jnp.dot(kern, right_cols, preferred_element_type=F32, precision=lax.Precision.HIGHEST))
    product = jnp.concatenate(parts, axis=1)
    total = contract_rows(lax.all_gather(mtx_left[0], "col", axis=0, tiled=True), product)
    return lax.psum(total, ("row", "col"))


def flip(value, mask):
    bit, out = 1, value
    while bit <= mask:
        if mask & bit:
            out = out + bit - 2 * bit * lax.rem(lax.div(value, bit), 2)
        bit *= 2
    return out


def split(x):
    high = x.astype(BF16)
    return high, (x - high.astype(F32)).astype(BF16)


def body(
    nrow, ncol, tile,
    ids, levels, evals, w_hbm, f_hbm, l_hbm, r_hbm, out,
    wbuf, fbuf, rbuf, lbuf, rsplit, acc, sigma, part, recv, gat,
    wsem, fsem, ownsem, rsend, rrecv, lsend, lrecv, ssend, srecv, gsend, grecv,
):
    ne = evals.shape[0]
    rows, depth = wbuf.shape[1:]
    lrows, ns = lbuf.shape[1:]
    n = nrow * ncol
    row, col = lax.axis_index("row"), lax.axis_index("col")
    me = row * ncol + col

    loads = []
    for s in range(nrow):
        cols = pl.ds(pl.multiple_of(flip(row, s) * depth, depth), depth)
        pair = [
            pltpu.make_async_copy(f_hbm.at[:, cols], fbuf.at[s], fsem.at[s]),
            pltpu.make_async_copy(w_hbm.at[:, cols], wbuf.at[s], wsem.at[s]),
        ]
        loads.append(pair)
    own = [
        pltpu.make_async_copy(r_hbm, rbuf.at[0], ownsem.at[0]),
        pltpu.make_async_copy(l_hbm, lbuf.at[0], ownsem.at[1]),
    ]

    barrier = pltpu.get_barrier_semaphore()

    @pl.loop(1, n)
    def _(d):
        peer = lax.rem(me + d, n)
        pl.semaphore_signal(barrier, inc=1, device_id=(lax.div(peer, ncol), lax.rem(peer, ncol)), device_id_type=MESH)

    own[0].start()
    for copy in loads[0]:
        copy.start()
    own[1].start()
    for pair in loads[1:]:
        for copy in pair:
            copy.start()
    pl.semaphore_wait(barrier, n - 1)

    rcopies = [None] + [
        pltpu.make_async_remote_copy(
            r_hbm, rbuf.at[s], rsend.at[s], rrecv.at[s],
            device_id=(flip(row, s), col), device_id_type=MESH,
        )
        for s in range(1, nrow)
    ]
    lcopies = [None] * ncol
    for d in range(1, ncol):
        direct = d == 1 or d % 2 == 0
        lcopies[d] = pltpu.make_async_remote_copy(
            l_hbm if direct else lbuf.at[d - 1], lbuf.at[d], lsend.at[d], lrecv.at[d],
            device_id=(row, flip(col, d if direct else 1)), device_id_type=MESH,
        )
    for copy in rcopies[1:]:
        copy.start()
    lcopies[1].start()
    for d in range(2, ncol, 2):
        lcopies[d].start()

    level = levels[ids[0]]
    shifts = [evals[k] - level for k in range(ne)]

    for s in range(nrow):
        if s == 0:
            own[0].wait()
        else:
            rcopies[s].wait_recv()
        high, low = split(rbuf[s])
        rsplit[:, :ns] = high
        rsplit[:, ns:] = low
        for copy in loads[s]:
            copy.wait()

        @pl.loop(0, rows // tile)
        def _(t):
            at = pl.ds(pl.multiple_of(t * tile, tile), tile)
            freq = fbuf[s, at, :]
            ratio = wbuf[s, at, :] * pltpu.reciprocal(freq, approx=True)
            both = rsplit[...]
            for k in range(ne):
                gap = shifts[k] - freq
                kern = ratio * gap * pltpu.reciprocal(gap * gap + 0.09, approx=True)
                high, low = split(kern)
                value = jnp.dot(high, both, preferred_element_type=F32) + jnp.dot(low, both, preferred_element_type=F32)
                if s == 0:
                    acc[k, at, :] = value
                else:
                    acc[k, at, :] += value

    own[1].wait()
    for d in range(2, ncol, 2):
        lcopies[d].wait_recv()
        lcopies[d + 1].start()
    lcopies[1].wait_recv()
    for d in range(2, ncol, 2):
        lcopies[d + 1].wait_recv()

    sigma[...] = jnp.zeros_like(sigma)
    for d in range(ncol):
        lhigh, llow = split(lbuf[d].T)
        left = jnp.concatenate([lhigh, llow], axis=0)
        at = pl.ds(pl.multiple_of(flip(col, d) * lrows, lrows), lrows)
        for k in range(ne):
            wide = acc[k, at, :]
            high, low = split(wide[:, :ns] + wide[:, ns:])
            top = jnp.dot(left, high, preferred_element_type=F32)
            more = jnp.dot(lhigh, low, preferred_element_type=F32)
            sigma[:, k * ns : (k + 1) * ns] += top[:ns] + top[ns:] + more

    size = part.shape[1]
    for p in range(n):
        part[p] = sigma[p * size : (p + 1) * size, :]

    def peer_of(d):
        peer = lax.rem(me + d, n)
        return peer, (lax.div(peer, ncol), lax.rem(peer, ncol))

    def scatter(d):
        peer, place = peer_of(d)
        return pltpu.make_async_remote_copy(
            part.at[peer], recv.at[d], ssend.at[d], srecv.at[d], device_id=place, device_id_type=MESH)

    def spread(d):
        _, place = peer_of(d)
        return pltpu.make_async_remote_copy(
            gat.at[me], gat.at[me], gsend.at[d], grecv.at[d], device_id=place, device_id_type=MESH)

    @pl.loop(1, n)
    def _(d):
        scatter(d).start()

    recv[0] = part[me]

    @pl.loop(1, n)
    def _(d):
        scatter(d).wait_recv()

    gat[me] = jnp.sum(recv[...], axis=0)

    @pl.loop(1, n)
    def _(d):
        spread(d).start()

    @pl.loop(1, n)
    def _(d):
        spread(d).wait_recv()

    for p in range(n):
        out[p * size : (p + 1) * size, :] = gat[p]

    for copy in rcopies[1:] + lcopies[1:]:
        copy.wait_send()

    @pl.loop(1, n)
    def _(d):
        scatter(d).wait_send()
        spread(d).wait_send()


def fused(nrow, ncol, tile, omega_sq, pole_freq, mtx_left, mtx_right, band_ids, band_energy, eval_energy):
    rows, cols = omega_sq.shape
    lrows, ns = mtx_left.shape[1:]
    rrows = mtx_right.shape[1]
    ne = eval_energy.shape[0]
    n = nrow * ncol
    size = ns // n
    dma = pltpu.SemaphoreType.DMA
    smem = pl.BlockSpec(memory_space=pltpu.SMEM)
    anywhere = pl.BlockSpec(memory_space=pl.ANY)
    return pl.pallas_call(
        functools.partial(body, nrow, ncol, tile),
        out_shape=jax.ShapeDtypeStruct((ns, ne * ns), F32),
        in_specs=[smem] * 3 + [anywhere] * 4,
        out_specs=pl.BlockSpec(memory_space=pltpu.VMEM),
        scratch_shapes=[
            pltpu.VMEM((nrow, rows, rrows), F32),
            pltpu.VMEM((nrow, rows, rrows), F32),
            pltpu.VMEM((nrow, rrows, ns), F32),
            pltpu.VMEM((ncol, lrows, ns), F32),
            pltpu.VMEM((rrows, 2 * ns), BF16),
            pltpu.VMEM((ne, rows, 2 * ns), F32),
            pltpu.VMEM((ns, ne * ns), F32),
            pltpu.VMEM((n, size, ne * ns), F32),
            pltpu.VMEM((n, size, ne * ns), F32),
            pltpu.VMEM((n, size, ne * ns), F32),
            dma((nrow,)), dma((nrow,)), dma((2,)),
            dma((nrow,)), dma((nrow,)), dma((ncol,)), dma((ncol,)),
            dma((n,)), dma((n,)), dma((n,)), dma((n,)),
        ],
        compiler_params=pltpu.CompilerParams(
            collective_id=0, has_side_effects=True, vmem_limit_bytes=48 * 1024 * 1024
        ),
        cost_estimate=pl.CostEstimate(
            flops=6 * rows * cols * ns * ne, bytes_accessed=8 * rows * cols, transcendentals=0
        ),
    )(band_ids, band_energy, eval_energy, omega_sq, pole_freq, mtx_left[0], mtx_right[0])


def shards(nrow, ncol, omega_sq, pole_freq, mtx_left, *rest):
    rows, cols = omega_sq.shape
    lrows, ns = mtx_left.shape[1:]
    n = nrow * ncol
    powers = nrow & (nrow - 1) == 0 and ncol & (ncol - 1) == 0 and ncol > 1
    fits = powers and ns % 128 == 0 and n <= ns and ns % n == 0 and lrows % 128 == 0
    fits = fits and cols % (128 * nrow) == 0 and rows * cols * 8 <= 16 * 1024 * 1024
    if not fits:
        return plain(omega_sq, pole_freq, mtx_left, *rest)
    return fused(nrow, ncol, 128, omega_sq, pole_freq, mtx_left, *rest)


def solution(mesh):
    return jax.shard_map(
        functools.partial(shards, mesh.shape["row"], mesh.shape["col"]),
        mesh=mesh,
        in_specs=(
            P("row", "col"),
            P("row", "col"),
            P(None, ("row", "col"), None),
            P(None, ("col", "row"), None),
            P(),
            P(),
            P(),
        ),
        out_specs=P(),
        check_vma=False,
    )
```

```python
import functools

import jax
import jax.numpy as jnp
from jax import lax
from jax.experimental import pallas as pl
from jax.experimental.pallas import tpu as pltpu
from jax.sharding import PartitionSpec as P

MESH = pl.DeviceIdType.MESH
F32 = jnp.float32
BF16 = jnp.bfloat16


def contract_rows(left, right):
    return lax.dot_general(
        left,
        right,
        (((0,), (0,)), ((), ())),
        precision=lax.Precision.HIGHEST,
        preferred_element_type=F32,
    )


def plain(omega_sq, pole_freq, mtx_left, mtx_right, band_ids, band_energy, eval_energy):
    shifts = eval_energy - band_energy[band_ids[0]]
    ratio = omega_sq / pole_freq
    right_cols = lax.all_gather(mtx_right[0], "row", axis=0, tiled=True)
    parts = []
    for energy in range(eval_energy.shape[0]):
        gap = shifts[energy] - pole_freq
        kern = ratio * gap / (gap * gap + 0.09)
        parts.append(jnp.dot(kern, right_cols, preferred_element_type=F32, precision=lax.Precision.HIGHEST))
    product = jnp.concatenate(parts, axis=1)
    total = contract_rows(lax.all_gather(mtx_left[0], "col", axis=0, tiled=True), product)
    return lax.psum(total, ("row", "col"))


def flip(value, mask):
    bit, out = 1, value
    while bit <= mask:
        if mask & bit:
            out = out + bit - 2 * bit * lax.rem(lax.div(value, bit), 2)
        bit *= 2
    return out


def split(x):
    high = x.astype(BF16)
    return high, (x - high.astype(F32)).astype(BF16)


def body(
    nrow, ncol, tile,
    ids_hbm, levels_hbm, evals_hbm, w_hbm, f_hbm, l_hbm, r_hbm, out,
    ids, levels, evals, wbuf, fbuf, rbuf, lbuf, rsplit, acc, sigma, theirs, mine, bands, pairs, joined, full,
    wsem, fsem, ownsem, rsend, rrecv, lsend, lrecv, ssend, srecv, gsend, grecv, asend, arecv, bsend, brecv, smallsem,
):
    ne = evals.shape[0]
    rows, depth = wbuf.shape[1:]
    lrows, ns = lbuf.shape[1:]
    row, col = lax.axis_index("row"), lax.axis_index("col")

    loads = []
    for s in range(nrow):
        cols = pl.ds(pl.multiple_of(flip(row, s) * depth, depth), depth)
        pair = [
            pltpu.make_async_copy(f_hbm.at[:, cols], fbuf.at[s], fsem.at[s]),
            pltpu.make_async_copy(w_hbm.at[:, cols], wbuf.at[s], wsem.at[s]),
        ]
        loads.append(pair)
    own = [
        pltpu.make_async_copy(r_hbm, rbuf.at[0], ownsem.at[0]),
        pltpu.make_async_copy(l_hbm, lbuf.at[0], ownsem.at[1]),
    ]

    small = [
        pltpu.make_async_copy(source, target, smallsem.at[i])
        for i, (source, target) in enumerate([(ids_hbm, ids), (levels_hbm, levels), (evals_hbm, evals)])
    ]
    for copy in small:
        copy.start()
    barrier = pltpu.get_barrier_semaphore()

    for d in range(1, nrow):
        pl.semaphore_signal(barrier, inc=1, device_id=(flip(row, d), col), device_id_type=MESH)
    for d in range(1, ncol):
        pl.semaphore_signal(barrier, inc=1, device_id=(row, flip(col, d)), device_id_type=MESH)

    own[0].start()
    for copy in loads[0]:
        copy.start()
    own[1].start()
    for pair in loads[1:]:
        for copy in pair:
            copy.start()
    pl.semaphore_wait(barrier, nrow + ncol - 2)

    rcopies = [None] + [
        pltpu.make_async_remote_copy(
            r_hbm, rbuf.at[s], rsend.at[s], rrecv.at[s],
            device_id=(flip(row, s), col), device_id_type=MESH,
        )
        for s in range(1, nrow)
    ]
    lcopies = [None] * ncol
    for d in range(1, ncol):
        direct = d == 1 or d % 2 == 0
        lcopies[d] = pltpu.make_async_remote_copy(
            l_hbm if direct else lbuf.at[d - 1], lbuf.at[d], lsend.at[d], lrecv.at[d],
            device_id=(row, flip(col, d if direct else 1)), device_id_type=MESH,
        )
    for copy in rcopies[1:]:
        copy.start()
    lcopies[1].start()
    for d in range(2, ncol, 2):
        lcopies[d].start()

    for copy in small:
        copy.wait()
    level = levels[ids[0]]
    shifts = [evals[k] - level for k in range(ne)]

    for s in range(nrow):
        if s == 0:
            own[0].wait()
        else:
            rcopies[s].wait_recv()
        high, low = split(rbuf[s])
        rsplit[:depth, :ns] = high
        rsplit[:depth, ns:] = low
        rsplit[depth:, :ns] = high
        rsplit[depth:, ns:] = low
        for copy in loads[s]:
            copy.wait()

        @pl.loop(0, rows // tile)
        def _(t):
            at = pl.ds(pl.multiple_of(t * tile, tile), tile)
            freq = fbuf[s, at, :]
            ratio = wbuf[s, at, :] * pltpu.reciprocal(freq, approx=True)
            both = rsplit[...]
            for k in range(ne):
                gap = shifts[k] - freq
                kern = ratio * gap * pltpu.reciprocal(gap * gap + 0.09, approx=True)
                high, low = split(kern)
                value = jnp.dot(jnp.concatenate([high, low], axis=1), both, preferred_element_type=F32)
                if s == 0:
                    acc[k, at, :] = value
                else:
                    acc[k, at, :] += value

    own[1].wait()
    sigma[...] = jnp.zeros_like(sigma)
    for d in [0, 1, *range(2, ncol, 2), *range(3, ncol, 2)]:
        if d:
            lcopies[d].wait_recv()
            if d % 2 == 0:
                lcopies[d + 1].start()
        lhigh, llow = split(lbuf[d].T)
        left = jnp.concatenate([lhigh, llow], axis=0)
        at = pl.ds(pl.multiple_of(flip(col, d) * lrows, lrows), lrows)
        for k in range(ne):
            wide = acc[k, at, :]
            high, low = split(wide[:, :ns] + wide[:, ns:])
            top = jnp.dot(left, high, preferred_element_type=F32)
            more = jnp.dot(lhigh, low, preferred_element_type=F32)
            sigma[:, k * ns : (k + 1) * ns] += top[:ns] + top[ns:] + more

    side, place = lax.rem(col, 2), lax.div(col, 2)
    half, piece = ns // 2, ns // 2 // nrow
    npair = ncol // 2

    def half_of(index):
        return pl.ds(pl.multiple_of(index * half, half), half)

    def piece_of(index):
        return pl.ds(pl.multiple_of(index * piece, piece), piece)

    def over_row(source, target, s, send, landed):
        return pltpu.make_async_remote_copy(
            source, target, send.at[s], landed.at[s], device_id=(flip(row, s), col), device_id_type=MESH)

    def over_col(source, target, d, send, landed):
        return pltpu.make_async_remote_copy(
            source, target, send.at[d], landed.at[d], device_id=(row, flip(col, d)), device_id_type=MESH)

    first = over_col(sigma.at[half_of(1 - side)], theirs, 1, ssend, srecv)
    first.start()
    first.wait_recv()
    mine[...] = sigma[half_of(side), :] + theirs[...]

    second = [over_row(mine.at[piece_of(flip(row, s))], bands.at[s], s, asend, arecv) for s in range(1, nrow)]
    for copy in second:
        copy.start()
    total = mine[piece_of(row), :]
    for s, copy in enumerate(second):
        copy.wait_recv()
        total += bands[s + 1]
    pairs[place] = total

    third = [over_col(pairs.at[place], pairs.at[place], d, gsend, grecv) for d in range(2, ncol, 2)]
    for copy in third:
        copy.start()
    for copy in third:
        copy.wait_recv()
    total = pairs[0]
    for p in range(1, npair):
        total += pairs[p]
    joined[piece_of(row), :] = total

    fourth = [over_row(joined.at[piece_of(row)], joined.at[piece_of(row)], s, bsend, brecv) for s in range(1, nrow)]
    for copy in fourth:
        copy.start()
    for copy in fourth:
        copy.wait_recv()

    fifth = over_col(joined, full, 1, gsend, grecv)
    fifth.start()
    out[half_of(side), :] = joined[...]
    fifth.wait_recv()
    out[half_of(1 - side), :] = full[...]

    for copy in rcopies[1:] + lcopies[1:] + [first] + second + third + fourth + [fifth]:
        copy.wait_send()


def fused(nrow, ncol, tile, omega_sq, pole_freq, mtx_left, mtx_right, band_ids, band_energy, eval_energy):
    rows, cols = omega_sq.shape
    lrows, ns = mtx_left.shape[1:]
    rrows = mtx_right.shape[1]
    ne = eval_energy.shape[0]
    dma = pltpu.SemaphoreType.DMA
    hbm = pl.BlockSpec(memory_space=pltpu.HBM)
    return pl.pallas_call(
        functools.partial(body, nrow, ncol, tile),
        out_shape=jax.ShapeDtypeStruct((ns, ne * ns), F32),
        in_specs=[hbm] * 7,
        out_specs=pl.BlockSpec(memory_space=pltpu.VMEM),
        scratch_shapes=[
            pltpu.SMEM(band_ids.shape, jnp.int32),
            pltpu.SMEM(band_energy.shape, F32),
            pltpu.SMEM(eval_energy.shape, F32),
            pltpu.VMEM((nrow, rows, rrows), F32),
            pltpu.VMEM((nrow, rows, rrows), F32),
            pltpu.VMEM((nrow, rrows, ns), F32),
            pltpu.VMEM((ncol, lrows, ns), F32),
            pltpu.VMEM((2 * rrows, 2 * ns), BF16),
            pltpu.VMEM((ne, rows, 2 * ns), F32),
            pltpu.VMEM((ns, ne * ns), F32),
            pltpu.VMEM((ns // 2, ne * ns), F32),
            pltpu.VMEM((ns // 2, ne * ns), F32),
            pltpu.VMEM((nrow, ns // 2 // nrow, ne * ns), F32),
            pltpu.VMEM((ncol // 2, ns // 2 // nrow, ne * ns), F32),
            pltpu.VMEM((ns // 2, ne * ns), F32),
            pltpu.VMEM((ns // 2, ne * ns), F32),
            dma((nrow,)), dma((nrow,)), dma((2,)),
            dma((nrow,)), dma((nrow,)), dma((ncol,)), dma((ncol,)),
            dma((ncol,)), dma((ncol,)), dma((ncol,)), dma((ncol,)),
            dma((nrow,)), dma((nrow,)), dma((nrow,)), dma((nrow,)), dma((3,)),
        ],
        compiler_params=pltpu.CompilerParams(
            collective_id=0, has_side_effects=True, vmem_limit_bytes=48 * 1024 * 1024
        ),
        cost_estimate=pl.CostEstimate(
            flops=6 * rows * cols * ns * ne, bytes_accessed=8 * rows * cols, transcendentals=0
        ),
    )(band_ids, band_energy, eval_energy, omega_sq, pole_freq, mtx_left[0], mtx_right[0])


def shards(nrow, ncol, omega_sq, pole_freq, mtx_left, *rest):
    rows, cols = omega_sq.shape
    lrows, ns = mtx_left.shape[1:]
    powers = nrow & (nrow - 1) == 0 and ncol & (ncol - 1) == 0 and ncol > 1
    fits = powers and rows % 1024 == 0 and ns % 128 == 0 and ns % (16 * nrow) == 0 and lrows % 128 == 0
    fits = fits and cols % (128 * nrow) == 0 and rows * cols * 8 <= 16 * 1024 * 1024
    if not fits:
        return plain(omega_sq, pole_freq, mtx_left, *rest)
    return fused(nrow, ncol, min(1024, rows), omega_sq, pole_freq, mtx_left, *rest)


def solution(mesh):
    return jax.shard_map(
        functools.partial(shards, mesh.shape["row"], mesh.shape["col"]),
        mesh=mesh,
        in_specs=(
            P("row", "col"),
            P("row", "col"),
            P(None, ("row", "col"), None),
            P(None, ("col", "row"), None),
            P(),
            P(),
            P(),
        ),
        out_specs=P(),
        check_vma=False,
    )
```

```python
import functools

import jax
import jax.numpy as jnp
from jax import lax
from jax.experimental import pallas as pl
from jax.experimental.pallas import tpu as pltpu
from jax.sharding import PartitionSpec as P

MESH = pl.DeviceIdType.MESH
F32 = jnp.float32
BF16 = jnp.bfloat16


def contract_rows(left, right):
    return lax.dot_general(
        left,
        right,
        (((0,), (0,)), ((), ())),
        precision=lax.Precision.HIGHEST,
        preferred_element_type=F32,
    )


def plain(omega_sq, pole_freq, mtx_left, mtx_right, band_ids, band_energy, eval_energy):
    shifts = eval_energy - band_energy[band_ids[0]]
    ratio = omega_sq / pole_freq
    right_cols = lax.all_gather(mtx_right[0], "row", axis=0, tiled=True)
    parts = []
    for energy in range(eval_energy.shape[0]):
        gap = shifts[energy] - pole_freq
        kern = ratio * gap / (gap * gap + 0.09)
        parts.append(jnp.dot(kern, right_cols, preferred_element_type=F32, precision=lax.Precision.HIGHEST))
    product = jnp.concatenate(parts, axis=1)
    total = contract_rows(lax.all_gather(mtx_left[0], "col", axis=0, tiled=True), product)
    return lax.psum(total, ("row", "col"))


def flip(value, mask):
    bit, out = 1, value
    while bit <= mask:
        if mask & bit:
            out = out + bit - 2 * bit * lax.rem(lax.div(value, bit), 2)
        bit *= 2
    return out


def split(x):
    high = x.astype(BF16)
    return high, (x - high.astype(F32)).astype(BF16)


def body(
    nrow, ncol, tile,
    ids_hbm, levels_hbm, evals_hbm, w_hbm, f_hbm, l_hbm, r_hbm, out,
    ids, levels, evals, wbuf, fbuf, rbuf, lbuf, rsplit, acc, sigma, theirs, mine, bands, pairs, joined, full,
    wsem, fsem, ownsem, rsend, rrecv, lsend, lrecv, ssend, srecv, gsend, grecv, asend, arecv, bsend, brecv, smallsem,
):
    ne = evals.shape[0]
    rows, depth = wbuf.shape[1:]
    lrows, ns = lbuf.shape[1:]
    row, col = lax.axis_index("row"), lax.axis_index("col")

    loads = []
    for s in range(nrow):
        cols = pl.ds(pl.multiple_of(flip(row, s) * depth, depth), depth)
        pair = [
            pltpu.make_async_copy(f_hbm.at[:, cols], fbuf.at[s], fsem.at[s]),
            pltpu.make_async_copy(w_hbm.at[:, cols], wbuf.at[s], wsem.at[s]),
        ]
        loads.append(pair)
    own = [
        pltpu.make_async_copy(r_hbm, rbuf.at[0], ownsem.at[0]),
        pltpu.make_async_copy(l_hbm, lbuf.at[0], ownsem.at[1]),
    ]

    small = [
        pltpu.make_async_copy(source, target, smallsem.at[i])
        for i, (source, target) in enumerate([(ids_hbm, ids), (levels_hbm, levels), (evals_hbm, evals)])
    ]
    for copy in small:
        copy.start()
    barrier = pltpu.get_barrier_semaphore()

    for d in range(1, nrow):
        pl.semaphore_signal(barrier, inc=1, device_id=(flip(row, d), col), device_id_type=MESH)
    for d in range(1, ncol):
        pl.semaphore_signal(barrier, inc=1, device_id=(row, flip(col, d)), device_id_type=MESH)

    own[0].start()
    for copy in loads[0]:
        copy.start()
    own[1].start()
    for pair in loads[1:]:
        for copy in pair:
            copy.start()
    pl.semaphore_wait(barrier, nrow + ncol - 2)

    rcopies = [None] + [
        pltpu.make_async_remote_copy(
            r_hbm, rbuf.at[s], rsend.at[s], rrecv.at[s],
            device_id=(flip(row, s), col), device_id_type=MESH,
        )
        for s in range(1, nrow)
    ]
    lcopies = [None] * ncol
    for d in range(1, ncol):
        relayed = d > 4 and d % 4 == 2
        if d == 1 or d % 2 == 0 and not relayed:
            source, mask = l_hbm, d
        elif relayed:
            source, mask = lbuf.at[d - 2], 2
        else:
            source, mask = lbuf.at[d - 1], 1
        lcopies[d] = pltpu.make_async_remote_copy(
            source, lbuf.at[d], lsend.at[d], lrecv.at[d],
            device_id=(row, flip(col, mask)), device_id_type=MESH,
        )
    early = [d for d in range(2, ncol, 2) if d == 2 or d % 4 == 0]
    late = [d for d in range(2, ncol, 2) if d not in early]
    for copy in rcopies[1:]:
        copy.start()
    for d in early[1:] + early[:1] + []:
        lcopies[d].start()
    lcopies[1].start()

    for copy in small:
        copy.wait()
    level = levels[ids[0]]
    shifts = [evals[k] - level for k in range(ne)]

    for s in range(nrow):
        if s == 0:
            own[0].wait()
        else:
            rcopies[s].wait_recv()
        high, low = split(rbuf[s])
        rsplit[:depth, :ns] = high
        rsplit[:depth, ns:] = low
        rsplit[depth:, :ns] = high
        rsplit[depth:, ns:] = low
        for copy in loads[s]:
            copy.wait()

        @pl.loop(0, rows // tile, unroll=True)
        def _(t):
            at = pl.ds(pl.multiple_of(t * tile, tile), tile)
            freq = fbuf[s, at, :]
            ratio = wbuf[s, at, :] * pltpu.reciprocal(freq, approx=True)
            both = rsplit[...]
            for k in range(ne):
                gap = shifts[k] - freq
                kern = ratio * gap * pltpu.reciprocal(gap * gap + 0.09, approx=True)
                high, low = split(kern)
                value = jnp.dot(jnp.concatenate([high, low], axis=1), both, preferred_element_type=F32)
                if s == 0:
                    acc[k, at, :] = value
                else:
                    acc[k, at, :] += value

        if s == min(1, nrow - 1):
            for d in early:
                lcopies[d].wait_recv()
                if d + 2 in late:
                    lcopies[d + 2].start()
                lcopies[d + 1].start()

    own[1].wait()
    sigma[...] = jnp.zeros_like(sigma)
    order = [0, 1, *early, *(d + 1 for d in early), *late, *(d + 1 for d in late)]
    for d in order:
        if d == 1 or d in late:
            lcopies[d].wait_recv()
            if d in late:
                lcopies[d + 1].start()
        elif d % 2:
            lcopies[d].wait_recv()
        lhigh, llow = split(lbuf[d].T)
        left = jnp.concatenate([lhigh, llow], axis=0)
        at = pl.ds(pl.multiple_of(flip(col, d) * lrows, lrows), lrows)
        for k in range(ne):
            wide = acc[k, at, :]
            high, low = split(wide[:, :ns] + wide[:, ns:])
            top = jnp.dot(left, high, preferred_element_type=F32)
            more = jnp.dot(lhigh, low, preferred_element_type=F32)
            sigma[:, k * ns : (k + 1) * ns] += top[:ns] + top[ns:] + more

    side, place = lax.rem(col, 2), lax.div(col, 2)
    half, piece = ns // 2, ns // 2 // nrow
    npair = ncol // 2

    def half_of(index):
        return pl.ds(pl.multiple_of(index * half, half), half)

    def piece_of(index):
        return pl.ds(pl.multiple_of(index * piece, piece), piece)

    def over_row(source, target, s, send, landed):
        return pltpu.make_async_remote_copy(
            source, target, send.at[s], landed.at[s], device_id=(flip(row, s), col), device_id_type=MESH)

    def over_col(source, target, d, send, landed):
        return pltpu.make_async_remote_copy(
            source, target, send.at[d], landed.at[d], device_id=(row, flip(col, d)), device_id_type=MESH)

    first = over_col(sigma.at[half_of(1 - side)], theirs, 1, ssend, srecv)
    first.start()
    first.wait_recv()
    mine[...] = sigma[half_of(side), :] + theirs[...]

    second = [over_row(mine.at[piece_of(flip(row, s))], bands.at[s], s, asend, arecv) for s in range(1, nrow)]
    for copy in second:
        copy.start()
    total = mine[piece_of(row), :]
    for s, copy in enumerate(second):
        copy.wait_recv()
        total += bands[s + 1]
    pairs[place] = total

    third = [over_col(pairs.at[place], pairs.at[place], d, gsend, grecv) for d in range(2, ncol, 2)]
    for copy in third:
        copy.start()
    for copy in third:
        copy.wait_recv()
    total = pairs[0]
    for p in range(1, npair):
        total += pairs[p]
    joined[piece_of(row), :] = total

    fourth = [over_row(joined.at[piece_of(row)], joined.at[piece_of(row)], s, bsend, brecv) for s in range(1, nrow)]
    for copy in fourth:
        copy.start()
    for copy in fourth:
        copy.wait_recv()

    fifth = over_col(joined, full, 1, gsend, grecv)
    fifth.start()
    out[half_of(side), :] = joined[...]
    fifth.wait_recv()
    out[half_of(1 - side), :] = full[...]

    for copy in rcopies[1:] + lcopies[1:] + [first] + second + third + fourth + [fifth]:
        copy.wait_send()


def fused(nrow, ncol, tile, omega_sq, pole_freq, mtx_left, mtx_right, band_ids, band_energy, eval_energy):
    rows, cols = omega_sq.shape
    lrows, ns = mtx_left.shape[1:]
    rrows = mtx_right.shape[1]
    ne = eval_energy.shape[0]
    dma = pltpu.SemaphoreType.DMA
    hbm = pl.BlockSpec(memory_space=pltpu.HBM)
    return pl.pallas_call(
        functools.partial(body, nrow, ncol, tile),
        out_shape=jax.ShapeDtypeStruct((ns, ne * ns), F32),
        in_specs=[hbm] * 7,
        out_specs=pl.BlockSpec(memory_space=pltpu.VMEM),
        scratch_shapes=[
            pltpu.SMEM(band_ids.shape, jnp.int32),
            pltpu.SMEM(band_energy.shape, F32),
            pltpu.SMEM(eval_energy.shape, F32),
            pltpu.VMEM((nrow, rows, rrows), F32),
            pltpu.VMEM((nrow, rows, rrows), F32),
            pltpu.VMEM((nrow, rrows, ns), F32),
            pltpu.VMEM((ncol, lrows, ns), F32),
            pltpu.VMEM((2 * rrows, 2 * ns), BF16),
            pltpu.VMEM((ne, rows, 2 * ns), F32),
            pltpu.VMEM((ns, ne * ns), F32),
            pltpu.VMEM((ns // 2, ne * ns), F32),
            pltpu.VMEM((ns // 2, ne * ns), F32),
            pltpu.VMEM((nrow, ns // 2 // nrow, ne * ns), F32),
            pltpu.VMEM((ncol // 2, ns // 2 // nrow, ne * ns), F32),
            pltpu.VMEM((ns // 2, ne * ns), F32),
            pltpu.VMEM((ns // 2, ne * ns), F32),
            dma((nrow,)), dma((nrow,)), dma((2,)),
            dma((nrow,)), dma((nrow,)), dma((ncol,)), dma((ncol,)),
            dma((ncol,)), dma((ncol,)), dma((ncol,)), dma((ncol,)),
            dma((nrow,)), dma((nrow,)), dma((nrow,)), dma((nrow,)), dma((3,)),
        ],
        compiler_params=pltpu.CompilerParams(
            collective_id=0, has_side_effects=True, vmem_limit_bytes=48 * 1024 * 1024
        ),
        cost_estimate=pl.CostEstimate(
            flops=6 * rows * cols * ns * ne, bytes_accessed=8 * rows * cols, transcendentals=0
        ),
    )(band_ids, band_energy, eval_energy, omega_sq, pole_freq, mtx_left[0], mtx_right[0])


def shards(nrow, ncol, omega_sq, pole_freq, mtx_left, *rest):
    rows, cols = omega_sq.shape
    lrows, ns = mtx_left.shape[1:]
    powers = nrow & (nrow - 1) == 0 and ncol & (ncol - 1) == 0 and ncol > 1
    fits = powers and rows % 1024 == 0 and ns % 128 == 0 and ns % (16 * nrow) == 0 and lrows % 128 == 0
    fits = fits and cols % (128 * nrow) == 0 and rows * cols * 8 <= 16 * 1024 * 1024
    if not fits:
        return plain(omega_sq, pole_freq, mtx_left, *rest)
    return fused(nrow, ncol, min(512, rows), omega_sq, pole_freq, mtx_left, *rest)


def solution(mesh):
    return jax.shard_map(
        functools.partial(shards, mesh.shape["row"], mesh.shape["col"]),
        mesh=mesh,
        in_specs=(
            P("row", "col"),
            P("row", "col"),
            P(None, ("row", "col"), None),
            P(None, ("col", "row"), None),
            P(),
            P(),
            P(),
        ),
        out_specs=P(),
        check_vma=False,
    )
```
